32 devices in a mesh: dp: 8 (over z, y), seq: 4 (over x, core).
Axes of the slice: x: 2, y: 2, z: 4, core: 2. Of those that a mesh axis runs over, the one named last changes fastest.
Arguments:
- tokens: bfloat16 [8, 1024, 768], P('dp', 'seq'), may hold values from -6 to 6
- conditioning: bfloat16 [8, 768], P('dp'), may hold values from -6 to 6
- cotangent: bfloat16 [8, 1024, 768], P('dp', 'seq'), may hold values from -6 to 6
- ada_weight: bfloat16 [2, 768, 4608], P(None, ('dp', 'seq')), may hold values from -0.21875 to 0.21875
- ada_bias: bfloat16 [2, 4608], P(None, ('dp', 'seq')), may hold values from -3 to 3
- qkv_weight: bfloat16 [2, 768, 2304], P(None, ('dp', 'seq')), may hold values from -0.21875 to 0.21875
- qv_bias: bfloat16 [2, 1536], P(None, ('dp', 'seq')), may hold values from -3 to 3
- proj_weight: bfloat16 [2, 768, 768], P(None, ('dp', 'seq')), may hold values from -0.875 to 0.875
- proj_bias: bfloat16 [2, 768], P(None, ('dp', 'seq')), may hold values from -2 to 2
- fc1_weight: bfloat16 [2, 768, 3072], P(None, ('dp', 'seq')), may hold values from -0.21875 to 0.21875
- fc1_bias: bfloat16 [2, 3072], P(None, ('dp', 'seq')), may hold values from -3 to 3
- fc2_weight: bfloat16 [2, 3072, 768], P(None, ('dp', 'seq')), may hold values from -0.109375 to 0.109375
- fc2_bias: bfloat16 [2, 768], P(None, ('dp', 'seq')), may hold values from -2 to 2
Outputs:
- block_out: float32 [8, 1024, 768], P('dp', 'seq')
- input_grad: float32 [8, 1024, 768], P('dp', 'seq')
- cond_grad: float32 [8, 768], P('dp')
- ada_weight_grad: float32 [2, 768, 4608], P(None, ('dp', 'seq'))
- ada_bias_grad: float32 [2, 4608], P(None, ('dp', 'seq'))
- qkv_weight_grad: float32 [2, 768, 2304], P(None, ('dp', 'seq'))
- qv_bias_grad: float32 [2, 1536], P(None, ('dp', 'seq'))
- proj_weight_grad: float32 [2, 768, 768], P(None, ('dp', 'seq'))
- proj_bias_grad: float32 [2, 768], P(None, ('dp', 'seq'))
- fc1_weight_grad: float32 [2, 768, 3072], P(None, ('dp', 'seq'))
- fc1_bias_grad: float32 [2, 3072], P(None, ('dp', 'seq'))
- fc2_weight_grad: float32 [2, 3072, 768], P(None, ('dp', 'seq'))
- fc2_bias_grad: float32 [2, 768], P(None, ('dp', 'seq'))
The draws below stay inside these ranges and needn't reach their ends.
All inputs are finite; a program needn't handle non-finite values.
Results may differ from the reference program's by a relative error of at most 0.019.
The reference program's roundings to bfloat16 on the way count: a program that leaves them out, or rounds other values in their place, can miss the bound.
Values may be sent and summed in bfloat16 or wider, within the bound.
A program may use at most 320 MiB of HBM per device.

```python
import jax
import jax.numpy as jnp
from jax import lax

D = 768
HEADS = 12
FF = 3072
HD = 64
LAYERS = 2
LEN = 1024
LAT = 8


def block_levels(own_key, extent, shards, low, largest):
    def one(position, blocks):
        draws = jax.random.uniform(jax.random.fold_in(jax.random.fold_in(own_key, 6), position), (blocks,), jnp.float32, low / len(shards), largest / len(shards))
        return jnp.repeat(jnp.exp(draws), extent[position] // blocks).reshape((-1,) + (1,) * (len(extent) - position - 1))

    loudness = one(*shards[0])
    for cut in shards[1:]:
        loudness = loudness * one(*cut)
    return loudness


def bell_draw(key, shape, scale, bound, pieces=(), held_as=jnp.bfloat16):
    level = block_levels(key, shape, pieces, -0.22, 0.18) if pieces else 1.0
    values = jax.random.normal(key, shape, jnp.float32) * scale * level
    return jnp.minimum(jnp.maximum(values, -bound), bound).astype(held_as)


def setup_inputs(seed: int = 0) -> dict:
    splits = jax.random.split(jax.random.key(seed), 14)
    return {
        "tokens": bell_draw(splits[0], (LAT, LEN, D), 1.0, 6.0, ((0, 8), (1, 4))),
        "conditioning": bell_draw(splits[1], (LAT, D), 1.0, 6.0, ((0, 8),)),
        "cotangent": bell_draw(splits[2], (LAT, LEN, D), 1.0, 6.0, ((0, 8), (1, 4))),
        "ada_weight": bell_draw(splits[3], (LAYERS, D, 6 * D), D ** -0.5, 0.21875, ((1, 32),)),
        "ada_bias": bell_draw(splits[4], (LAYERS, 6 * D), 0.5, 3.0, ((1, 32),)),
        "qkv_weight": bell_draw(splits[5], (LAYERS, D, 3 * D), D ** -0.5, 0.21875, ((1, 32),)),
        "qv_bias": bell_draw(splits[6], (LAYERS, 2 * D), 0.5, 3.0, ((1, 32),)),
        "proj_weight": bell_draw(splits[7], (LAYERS, D, D), (D // 16) ** -0.5, 0.875, ((1, 32),)),
        "proj_bias": bell_draw(splits[8], (LAYERS, D), 0.3, 2.0, ((1, 32),)),
        "fc1_weight": bell_draw(splits[9], (LAYERS, D, FF), D ** -0.5, 0.21875, ((1, 32),)),
        "fc1_bias": bell_draw(splits[10], (LAYERS, FF), 0.5, 3.0, ((1, 32),)),
        "fc2_weight": bell_draw(splits[11], (LAYERS, FF, D), FF ** -0.5, 0.109375, ((1, 32),)),
        "fc2_bias": bell_draw(splits[12], (LAYERS, D), 0.3, 2.0, ((1, 32),)),
    }


@jax.custom_vjp
def low(v):
    return lax.optimization_barrier(v.astype(jnp.bfloat16)).astype(jnp.float32)

@jax.custom_vjp
def low_back(v):
    return v

def low_keep(v):
    return (low(v), None)

def low_pass(kept, grad):
    return (grad,)

def back_keep(v):
    return (v, None)

def back_low(kept, grad):
    return (low(grad),)
low.defvjp(low_keep, low_pass)
low_back.defvjp(back_keep, back_low)
epsilon = 1e-06
highest = lax.Precision.HIGHEST

def layer_norm(values):
    center = values - lax.optimization_barrier(jnp.mean(values, axis=-1, keepdims=True))
    spread = lax.optimization_barrier(jnp.mean(center * center, axis=-1, keepdims=True))
    return center * lax.rsqrt(spread + epsilon)

def forward_latent(params, latent_tokens, latent_cond):
    cond_low = low(jax.nn.silu(latent_cond))
    resid = latent_tokens
    score_scale = HD ** (-0.5)
    for layer_at in range(LAYERS):
        ada_w, ada_b, qkv_w, qv_b, proj_w, proj_b, fc1_w, fc1_b, fc2_w, fc2_b = [member[layer_at] for member in params]
        mods = low_back(jnp.dot(cond_low, ada_w, precision=highest) + ada_b).reshape(6, D)
        attn_in = low(layer_norm(resid) * (1.0 + mods[1]) + mods[0])
        bias_full = jnp.concatenate([qv_b[:D], jnp.zeros((D,), jnp.float32), qv_b[D:]])
        joined = low_back(low(jnp.dot(attn_in, qkv_w, precision=highest) + bias_full))
        joined = joined.reshape(LEN, 3, HEADS, HD)
        queries, keys_in, values_in = (joined[:, 0], joined[:, 1], joined[:, 2])
        scores = low_back(jnp.einsum('qhe,khe->hqk', queries, keys_in, precision=highest) * score_scale)
        probability = jax.nn.softmax(scores, axis=-1)
        attended = jnp.einsum('hqk,khe->qhe', low(probability), values_in, precision=highest)
        attended = low_back(low(attended)).reshape(LEN, D)
        branch = low_back(jnp.dot(attended, proj_w, precision=highest) + proj_b)
        middle = resid + mods[2] * branch
        mlp_in = low(layer_norm(middle) * (1.0 + mods[4]) + mods[3])
        hidden_pre = low_back(jnp.dot(mlp_in, fc1_w, precision=highest) + fc1_b)
        hidden_act = low(jax.nn.gelu(hidden_pre, approximate=True))
        mlp_out = low_back(jnp.dot(hidden_act, fc2_w, precision=highest) + fc2_b)
        resid = middle + mods[5] * mlp_out
    return resid

def reference(tokens, conditioning, cotangent, ada_weight, ada_bias, qkv_weight, qv_bias, proj_weight, proj_bias, fc1_weight, fc1_bias, fc2_weight, fc2_bias):
    params = tuple((member.astype(jnp.float32) for member in (ada_weight, ada_bias, qkv_weight, qv_bias, proj_weight, proj_bias, fc1_weight, fc1_bias, fc2_weight, fc2_bias)))

    def latent_step(carry, item):
        latent_tokens, latent_cond, latent_cot = item
        result, pullback = jax.vjp(forward_latent, params, latent_tokens.astype(jnp.float32), latent_cond.astype(jnp.float32))
        grads, grad_tokens, grad_cond = pullback(latent_cot.astype(jnp.float32))
        carry = jax.tree.map(jnp.add, carry, grads)
        return (carry, (result, grad_tokens, grad_cond))
    initial = tuple((jnp.zeros_like(member) for member in params))
    grads, stacked = lax.scan(latent_step, initial, (tokens, conditioning, cotangent))
    block_out, input_grad, cond_grad = stacked
    return (block_out, input_grad, cond_grad, grads[0], grads[1], grads[2], grads[3], grads[4], grads[5], grads[6], grads[7], grads[8], grads[9])
```

```python
import jax
import jax.numpy as jnp
from jax import lax
from jax.sharding import PartitionSpec as P

HD = 64


BOTH = ("dp", "seq")


def gather_rows(share):
    return lax.all_gather(share, BOTH, axis=0, tiled=True)


def scatter_rows(grad):
    return lax.psum_scatter(grad, BOTH, scatter_dimension=0, tiled=True)


def exchange_rows(grad):
    groups, members = lax.axis_size("dp"), lax.axis_size("seq")
    me = lax.axis_index("seq")
    cut = grad.reshape(groups, members, -1, grad.shape[1])
    total = lax.dynamic_index_in_dim(cut, me, 1, False)
    for step in range(1, members):
        share = lax.dynamic_index_in_dim(cut, me ^ step, 1, False).astype(jnp.bfloat16)
        came = lax.ppermute(share, "seq", [(at, at ^ step) for at in range(members)])
        total = total + came.astype(jnp.float32)
    came = lax.all_to_all(
        total.astype(jnp.bfloat16), "dp", split_axis=0, concat_axis=0, tiled=True
    )
    return jnp.sum(came.astype(jnp.float32), axis=0)


epsilon = 1e-06


def layer_norm(values):
    center = values - jnp.mean(values, axis=-1, keepdims=True)
    spread = jnp.mean(center * center, axis=-1, keepdims=True)
    return center * lax.rsqrt(spread + epsilon)


def norm_back(values, grad):
    return jax.vjp(layer_norm, values)[1](grad)[0]


def gelu_tanh(values):
    return jax.nn.gelu(values, approximate=True)


def gelu_back(values, grad):
    return jax.vjp(gelu_tanh, values)[1](grad)[0]


def project(left, weight):
    return jnp.einsum("btd,de->bte", left, weight, preferred_element_type=jnp.float32)


def project_back(grad, weight):
    return jnp.einsum("bte,de->btd", grad, weight, preferred_element_type=jnp.float32)


def outer_sum(left, grad):
    return jnp.einsum("btd,bte->de", left, grad, preferred_element_type=jnp.float32)


def column_sums(grad):
    return jnp.sum(grad.astype(jnp.float32), axis=(0, 1))


def attention_one(heads):
    length, _, inner = heads.shape
    pieces = heads.reshape(length, 3, inner // HD, HD)
    queries, keys_in, values_in = (pieces[:, 0], pieces[:, 1], pieces[:, 2])
    scores = jnp.einsum(
        "qhe,khe->hqk", queries, keys_in, preferred_element_type=jnp.float32
    ) * HD ** (-0.5)
    row_max = jnp.max(scores, axis=-1, keepdims=True)
    exponent = jnp.exp(scores - row_max)
    row_sum = jnp.sum(exponent, axis=-1, keepdims=True)
    probability = (exponent / row_sum).astype(jnp.bfloat16)
    log_total = row_max + jnp.log(row_sum)
    result = jnp.einsum("hqk,khe->qhe", probability, values_in, preferred_element_type=jnp.float32)
    return (result.astype(jnp.bfloat16).reshape(length, inner), log_total)


def attention(heads):
    return lax.map(attention_one, heads)


def attention_back_one(item):
    heads, log_total, grad_heads = item
    length, _, inner = heads.shape
    pieces = heads.reshape(length, 3, inner // HD, HD)
    queries, keys_in, values_in = (pieces[:, 0], pieces[:, 1], pieces[:, 2])
    grad_out = grad_heads.reshape(length, inner // HD, HD)
    score_scale = HD ** (-0.5)
    scores = (
        jnp.einsum("qhe,khe->hqk", queries, keys_in, preferred_element_type=jnp.float32)
        * score_scale
    )
    probability = jnp.exp(scores - log_total)
    grad_prob = jnp.einsum("qhe,khe->hqk", grad_out, values_in, preferred_element_type=jnp.float32)
    row_dot = jnp.sum(probability * grad_prob, axis=-1, keepdims=True)
    grad_scores = (probability * (grad_prob - row_dot)).astype(jnp.bfloat16)
    grad_q = (
        jnp.einsum("hqk,khe->qhe", grad_scores, keys_in, preferred_element_type=jnp.float32)
        * score_scale
    )
    grad_k = (
        jnp.einsum("hqk,qhe->khe", grad_scores, queries, preferred_element_type=jnp.float32)
        * score_scale
    )
    grad_v = jnp.einsum(
        "hqk,qhe->khe",
        probability.astype(jnp.bfloat16),
        grad_out,
        preferred_element_type=jnp.float32,
    )
    stacked = jnp.stack([grad_q, grad_k, grad_v], axis=1).astype(jnp.bfloat16)
    return stacked.reshape(length, 3, inner)


def attention_back(heads, log_total, grad_heads):
    return lax.map(attention_back_one, (heads, log_total, grad_heads))


def forward_layer(params, resid, mods):
    qkv_w, qv_b, proj_w, proj_b, fc1_w, fc1_b, fc2_w, fc2_b = params
    width = resid.shape[2]
    attn_in = (layer_norm(resid) * (1.0 + mods[:, 1]) + mods[:, 0]).astype(jnp.bfloat16)
    query_bias = qv_b[:width].astype(jnp.float32)
    value_bias = qv_b[width:].astype(jnp.float32)
    bias_full = jnp.concatenate([query_bias, jnp.zeros((width,), jnp.float32), value_bias])
    joined = (project(attn_in, qkv_w) + bias_full).astype(jnp.bfloat16)
    joined = joined.reshape(resid.shape[0], resid.shape[1], 3, width)
    heads = lax.all_to_all(joined, "seq", split_axis=3, concat_axis=1, tiled=True)
    attended, log_total = attention(heads)
    attn_tok = lax.all_to_all(attended, "seq", split_axis=1, concat_axis=2, tiled=True)
    branch = project(attn_tok, proj_w) + proj_b.astype(jnp.float32)
    middle = resid + mods[:, 2] * branch
    mlp_in = (layer_norm(middle) * (1.0 + mods[:, 4]) + mods[:, 3]).astype(jnp.bfloat16)
    hidden_pre = project(mlp_in, fc1_w) + fc1_b.astype(jnp.float32)
    hidden_act = gelu_tanh(hidden_pre).astype(jnp.bfloat16)
    mlp_out = project(hidden_act, fc2_w) + fc2_b.astype(jnp.float32)
    result = middle + mods[:, 5] * mlp_out
    kept = (
        resid,
        attn_in,
        heads,
        log_total,
        attn_tok,
        branch,
        middle,
        mlp_in,
        hidden_pre,
        hidden_act,
        mlp_out,
    )
    return (result, kept)


def backward_layer(params, kept, grad_new, mods):
    (
        resid,
        attn_in,
        heads,
        log_total,
        attn_tok,
        branch,
        middle,
        mlp_in,
        hidden_pre,
        hidden_act,
        mlp_out,
    ) = kept
    qkv_w, qv_b, proj_w, proj_b, fc1_w, fc1_b, fc2_w, fc2_b = params
    latents, rows, width = resid.shape
    grad_mlp = (grad_new * mods[:, 5]).astype(jnp.bfloat16)
    grad_fc2_w = outer_sum(hidden_act, grad_mlp)
    grad_fc2_b = column_sums(grad_mlp)
    grad_hidden = project_back(grad_mlp, fc2_w)
    grad_pre = gelu_back(hidden_pre, grad_hidden).astype(jnp.bfloat16)
    grad_fc1_w = outer_sum(mlp_in, grad_pre)
    grad_fc1_b = column_sums(grad_pre)
    grad_mlp_in = project_back(grad_pre, fc1_w)
    normed_mid = layer_norm(middle)
    grad_shift_m = jnp.sum(grad_mlp_in, axis=1)
    grad_scale_m = jnp.sum(grad_mlp_in * normed_mid, axis=1)
    grad_gate_m = jnp.sum(grad_new * mlp_out, axis=1)
    grad_middle = grad_new + norm_back(middle, grad_mlp_in * (1.0 + mods[:, 4]))
    grad_gate_a = jnp.sum(grad_middle * branch, axis=1)
    grad_branch = (grad_middle * mods[:, 2]).astype(jnp.bfloat16)
    grad_proj_w = outer_sum(attn_tok, grad_branch)
    grad_proj_b = column_sums(grad_branch)
    grad_attended = project_back(grad_branch, proj_w).astype(jnp.bfloat16)
    grad_heads = lax.all_to_all(grad_attended, "seq", split_axis=2, concat_axis=1, tiled=True)
    grad_joined_heads = attention_back(heads, log_total, grad_heads)
    grad_joined = lax.all_to_all(grad_joined_heads, "seq", split_axis=1, concat_axis=3, tiled=True)
    grad_joined = grad_joined.reshape(latents, rows, 3 * width)
    grad_qkv_w = outer_sum(attn_in, grad_joined)
    joined_sums = column_sums(grad_joined)
    grad_qv_b = jnp.concatenate([joined_sums[:width], joined_sums[2 * width :]])
    grad_attn_in = project_back(grad_joined, qkv_w)
    normed_in = layer_norm(resid)
    grad_shift_a = jnp.sum(grad_attn_in, axis=1)
    grad_scale_a = jnp.sum(grad_attn_in * normed_in, axis=1)
    grad_resid = grad_middle + norm_back(resid, grad_attn_in * (1.0 + mods[:, 1]))
    grad_mods = jnp.stack(
        [grad_shift_a, grad_scale_a, grad_gate_a, grad_shift_m, grad_scale_m, grad_gate_m], axis=1
    )
    grad_mods = grad_mods.reshape(latents, 6 * width)
    grads = (
        grad_qkv_w,
        grad_qv_b,
        grad_proj_w,
        grad_proj_b,
        grad_fc1_w,
        grad_fc1_b,
        grad_fc2_w,
        grad_fc2_b,
    )
    return (grad_resid, grads, grad_mods)


def on_device(
    tokens,
    conditioning,
    cotangent,
    ada_weight,
    ada_bias,
    qkv_weight,
    qv_bias,
    proj_weight,
    proj_bias,
    fc1_weight,
    fc1_bias,
    fc2_weight,
    fc2_bias,
):
    layers = ada_weight.shape[0]
    width = conditioning.shape[1]
    latents = conditioning.shape[0]
    group = lax.axis_index("dp")
    owner = lax.axis_index(BOTH)
    own_rows = ada_weight.shape[1]
    cond_f32 = conditioning.astype(jnp.float32)
    cond_low = jax.nn.silu(cond_f32).astype(jnp.bfloat16)
    cond_every = lax.all_gather(cond_low, "dp", axis=0, tiled=True)
    cond_rows = lax.dynamic_slice_in_dim(cond_every, owner * own_rows, own_rows, 1)
    everyone = cond_every.shape[0]

    shares = (ada_bias, qv_bias, proj_bias, fc1_bias, fc2_bias)
    spread = [
        lax.dynamic_update_slice_in_dim(
            jnp.zeros((layers, share.shape[1] * lax.axis_size(BOTH)), jnp.float32),
            share.astype(jnp.float32),
            owner * share.shape[1],
            1,
        )
        for share in shares
    ]
    partial = jnp.einsum(
        "bd,ldm->lbm", cond_rows, ada_weight, preferred_element_type=jnp.float32
    )
    packed = jnp.concatenate(
        [partial.reshape(layers, -1)] + spread, axis=1
    )
    summed = lax.psum(packed, BOTH)
    modulated = summed[:, : partial.shape[1] * partial.shape[2]].reshape(partial.shape)
    at = partial.shape[1] * partial.shape[2]
    whole = []
    for one in spread:
        whole.append(summed[:, at : at + one.shape[1]])
        at += one.shape[1]
    mods_own = lax.dynamic_slice_in_dim(modulated, group * latents, latents, 1)
    mods_own = mods_own + whole[0][:, None]

    resid = tokens.astype(jnp.float32)
    kept_all = []
    params_all = []
    mods_all = []
    for layer_at in range(layers):
        params = (
            gather_rows(qkv_weight[layer_at]),
            whole[1][layer_at],
            gather_rows(proj_weight[layer_at]),
            whole[2][layer_at],
            gather_rows(fc1_weight[layer_at]),
            whole[3][layer_at],
            gather_rows(fc2_weight[layer_at]),
            whole[4][layer_at],
        )
        mods = mods_own[layer_at].reshape(latents, 6, 1, width)
        resid, kept = forward_layer(params, resid, mods)
        params_all.append(params)
        kept_all.append(kept)
        mods_all.append(mods)
    grad_resid = cotangent.astype(jnp.float32)
    owned = [None] * layers
    small = [None] * layers
    mods_sums = [None] * layers
    for layer_at in reversed(range(layers)):
        grad_resid, grads, mods_sums[layer_at] = backward_layer(
            params_all[layer_at], kept_all[layer_at], grad_resid, mods_all[layer_at]
        )
        owned[layer_at] = [exchange_rows(grads[member]) for member in (0, 2, 4)]
        owned[layer_at].append(scatter_rows(grads[6]))
        small[layer_at] = jnp.concatenate([grads[member] for member in (1, 3, 5, 7)])

    mods_sum = jnp.stack(mods_sums)
    mods_spread = lax.dynamic_update_slice_in_dim(
        jnp.zeros((layers, everyone, mods_sum.shape[2]), jnp.float32), mods_sum, group * latents, 1
    )
    total = lax.psum(
        jnp.concatenate([mods_spread.reshape(layers, -1), jnp.stack(small)], axis=1), BOTH
    )
    cut = mods_spread.shape[1] * mods_spread.shape[2]
    mods_every = total[:, :cut].reshape(mods_spread.shape).astype(jnp.bfloat16)
    ada_w_grad = jnp.einsum(
        "bd,lbm->ldm", cond_rows, mods_every, preferred_element_type=jnp.float32
    )
    mods_total = jnp.sum(mods_every.astype(jnp.float32), axis=1)
    ada_b_grad = lax.dynamic_slice_in_dim(
        mods_total, owner * ada_bias.shape[1], ada_bias.shape[1], 1
    )
    bias_grads = []
    for share in shares[1:]:
        bias_grads.append(
            lax.dynamic_slice_in_dim(total, cut + owner * share.shape[1], share.shape[1], 1)
        )
        cut += share.shape[1] * lax.axis_size(BOTH)
    cond_part = jnp.einsum(
        "lbm,ldm->bd", mods_every, ada_weight, preferred_element_type=jnp.float32
    )
    cond_all = lax.all_gather(cond_part, BOTH, axis=1, tiled=True)
    grad_cond = lax.dynamic_slice_in_dim(cond_all, group * latents, latents, 0)
    weight_grads = [
        jnp.stack([owned[layer_at][member] for layer_at in range(layers)]) for member in range(4)
    ]
    cond_out = jax.vjp(jax.nn.silu, cond_f32)[1](grad_cond)[0]
    return (
        resid,
        grad_resid,
        cond_out,
        ada_w_grad,
        ada_b_grad,
        weight_grads[0],
        bias_grads[0],
        weight_grads[1],
        bias_grads[1],
        weight_grads[2],
        bias_grads[2],
        weight_grads[3],
        bias_grads[3],
    )


def solution(mesh):
    placed = (
        P("dp", "seq", None),
        P("dp", None),
        P("dp", "seq", None),
        P(None, ("dp", "seq"), None),
        P(None, ("dp", "seq")),
        P(None, ("dp", "seq"), None),
        P(None, ("dp", "seq")),
        P(None, ("dp", "seq"), None),
        P(None, ("dp", "seq")),
        P(None, ("dp", "seq"), None),
        P(None, ("dp", "seq")),
        P(None, ("dp", "seq"), None),
        P(None, ("dp", "seq")),
    )
    return jax.shard_map(
        on_device,
        mesh=mesh,
        in_specs=placed,
        out_specs=(
            P("dp", "seq", None),
            P("dp", "seq", None),
            P("dp", None),
            P(None, ("dp", "seq"), None),
            P(None, ("dp", "seq")),
            P(None, ("dp", "seq"), None),
            P(None, ("dp", "seq")),
            P(None, ("dp", "seq"), None),
            P(None, ("dp", "seq")),
            P(None, ("dp", "seq"), None),
            P(None, ("dp", "seq")),
            P(None, ("dp", "seq"), None),
            P(None, ("dp", "seq")),
        ),
        check_vma=False,
    )
```
